128 devices in a mesh: dp: 32 (over x, z, core), seq: 4 (over y).
Axes of the slice: x: 4, y: 4, z: 4, core: 2. Of those that a mesh axis runs over, the one named last changes fastest.
Arguments:
- rewards: float32 [65536, 4096], P(('dp', 'seq')), may hold values from -21 to 21
- lengths: int32 [65536], P(('dp', 'seq')), may hold values from 512 to 4096
- prompt_ids: int32 [65536], P(('dp', 'seq')), may hold values from 0 to 4095, as said below
Outputs:
- advantage: float32 [65536, 4096], P(('dp', 'seq'))
- prompt_mean: float32 [4096], P('dp')
- prompt_var: float32 [4096], P('dp')
The draws below stay inside these ranges and needn't reach their ends.
Inputs may be any that keep to these rules, and one draw needn't show every extreme that they name: `prompt_ids`: each prompt id is named by exactly 16 completions. Every aligned block of 512 completions holds exactly 16 completions of the prompts o * 128 to (o + 1) * 128 - 1, for every o.
All inputs are finite; a program needn't handle non-finite values.
Results may differ from the reference program's by a relative error of at most 0.00011.
Values sent between devices are 32-bit elements; how exact they have to be, the bound alone decides.
No kernel may reach another device: no remote copies, remote signals or barrier semaphores. Data moves between devices by JAX's collectives and lax.ppermute only.
A program may use at most 64 MiB of HBM per device.

```python
import jax
import jax.numpy as jnp
from jax import lax

GROUP = 16
SAMP_DEV = 2048
LEN = 4096
P_DEV = 128
PER_PEER = 16
PROMPTS = 4096
COMPL = 65536
N_DP = 32
N_SEQ = 4


def shuffle_owners(subkey):
    return jax.random.permutation(subkey, jnp.arange(SAMP_DEV // N_SEQ, dtype=jnp.int32) % N_DP)


def shuffle_slots(subkey):
    return jax.random.permutation(subkey, jnp.arange(SAMP_DEV, dtype=jnp.int32))


def draw_prompt_ids(key, part):
    first_key = jax.random.fold_in(key, 11)
    second_key = jax.random.fold_in(key, 23)
    blocks = N_DP * N_SEQ
    owners = jax.vmap(shuffle_owners)(jax.random.split(first_key, blocks))
    hits = (owners[:, :, None] == jnp.arange(N_DP, dtype=jnp.int32)[None, None, :]).astype(jnp.int32)
    ranks = jnp.sum((jnp.cumsum(hits, axis=1) - hits) * hits, axis=2)
    position = jnp.arange(blocks, dtype=jnp.int32)[:, None] * PER_PEER + ranks
    tables = jax.vmap(shuffle_slots)(jax.random.split(second_key, N_DP))
    local_slot = tables[owners, position]
    return (owners * P_DEV + local_slot // GROUP).reshape(-1).astype(jnp.int32)


def draw_rewards(key, part):
    offset_key = jax.random.fold_in(key, 31)
    scale_key = jax.random.fold_in(key, 37)
    noise_key = jax.random.fold_in(key, 41)
    offset = jax.random.truncated_normal(offset_key, -3.0, 3.0, (COMPL, 1), jnp.float32)
    scale = jnp.exp(jax.random.uniform(scale_key, (COMPL, 1), jnp.float32, jnp.log(0.3), jnp.log(3.0)))
    noise = jax.random.truncated_normal(noise_key, -6.0, 6.0, (COMPL, LEN), jnp.float32)
    return (offset + scale * noise).astype(jnp.float32)


def set_ends(drawn, rng, low, high):
    longest = drawn.shape.index(max(drawn.shape))
    spots = []
    for shift in (0, 1):
        where = [jax.random.randint(jax.random.fold_in(rng, axis), (), 0, length) for axis, length in enumerate(drawn.shape)]
        where[longest] = (where[longest] + shift) % drawn.shape[longest]
        spots.append(tuple(where))
    return drawn.at[spots[0]].set(low).at[spots[1]].set(high)


def setup_inputs(seed: int = 0) -> dict:
    seeds = jax.random.split(jax.random.key(seed), 4)
    rewards = draw_rewards(jax.random.fold_in(seeds[3], 71), 0)
    lengths = set_ends(jax.random.randint(seeds[1], (COMPL,), LEN // 8, LEN + 1), jax.random.fold_in(seeds[1], 1), LEN // 8, LEN).astype(jnp.int32)
    prompt_ids = draw_prompt_ids(jax.random.fold_in(seeds[3], 71), 0)
    return dict(rewards=rewards, lengths=lengths, prompt_ids=prompt_ids)


EPSILON = 1e-06

def reference(rewards, lengths, prompt_ids):
    positions = jnp.arange(LEN, dtype=jnp.int32)
    valid = positions[None, :] < lengths[:, None]
    masked = jnp.where(valid, rewards, 0.0)
    counts = jax.ops.segment_sum(lengths.astype(jnp.float32), prompt_ids, num_segments=PROMPTS)
    totals = jax.ops.segment_sum(lax.optimization_barrier(jnp.sum(masked, axis=1)), prompt_ids, num_segments=PROMPTS)
    prompt_mean = totals / counts
    centred = jnp.where(valid, rewards - prompt_mean[prompt_ids][:, None], 0.0)
    squares = jax.ops.segment_sum(lax.optimization_barrier(jnp.sum(centred * centred, axis=1)), prompt_ids, num_segments=PROMPTS)
    prompt_var = squares / counts
    inv_std = lax.rsqrt(prompt_var + EPSILON)
    advantage = centred * inv_std[prompt_ids][:, None]
    return (advantage, prompt_mean, prompt_var)
```

```python
import jax
import jax.numpy as jnp
from jax import lax
from jax.experimental import pallas as pl
from jax.experimental.pallas import tpu as pltpu
from jax.sharding import Mesh
from jax.sharding import PartitionSpec as P

P_DEV = 128
OWNERS = 32
SEG = 16
LANES = 128
DP = ("dp_0", "dp_1", "dp_2")
DP_SEQ = ("dp_0", "dp_1", "dp_2", "seq")
CHIPS = ("dp_0", "dp_1", "seq")
EPSILON = 1e-06
MIB = 1024 * 1024
SURE = 4

PARTS = 4
VALUES = 4
ROWS_MSG = PARTS * VALUES


def lane_of(shape):
    return lax.broadcasted_iota(jnp.int32, shape, len(shape) - 1)


def spin(x, k):
    k %= SEG
    if k == 0:
        return x
    near = pltpu.roll(x, LANES - k, 1)
    wrapped = pltpu.roll(x, SEG - k, 1)
    return jnp.where(lane_of(x.shape) % SEG < SEG - k, near, wrapped)


def stats_kernel(chunk, rewards, lengths, ids, kept, message, packed, columns, sem):
    rows, width = rewards.shape
    groups = rows // LANES
    tiles = width // LANES
    chunks = rows // chunk

    def fetch(b):
        where = pl.ds(pl.multiple_of(b * chunk, chunk), chunk)
        return pltpu.make_async_copy(rewards.at[where], kept.at[where], sem.at[b])

    for b in range(chunks):
        fetch(b).start()

    both = jnp.concatenate([lengths[...], ids[...]], axis=0).astype(jnp.float32)
    turned = both.T
    owner_row = ids[...] >> 7
    lane = lane_of((LANES, LANES))
    below = lane < lax.broadcasted_iota(jnp.int32, (LANES, LANES), 0)
    sorted_ids = [jnp.zeros((8, LANES), jnp.float32) for _ in range(PARTS)]
    sorted_counts = [jnp.zeros((8, LANES), jnp.float32) for _ in range(PARTS)]
    for g in range(groups):
        length = jnp.broadcast_to(turned[:, g : g + 1], (LANES, LANES))
        prompt = jnp.broadcast_to(turned[:, groups + g : groups + g + 1], (LANES, LANES))
        owner = prompt.astype(jnp.int32) >> 7
        earlier = jnp.where((owner == owner_row[g : g + 1, :]) & below, 1.0, 0.0)
        for h in range(g):
            earlier += jnp.where(owner == owner_row[h : h + 1, :], 1.0, 0.0)
        rank = jnp.sum(earlier, axis=1, keepdims=True)
        slot = owner * SEG + rank.astype(jnp.int32)
        columns[0, g * LANES : (g + 1) * LANES, :] = slot
        columns[1, g * LANES : (g + 1) * LANES, :] = length.astype(jnp.int32)
        for s in range(PARTS):
            here = slot == lane + s * LANES
            sorted_ids[s] += jnp.sum(jnp.where(here, prompt, 0.0).reshape(LANES // 8, 8, LANES), axis=0)
            sorted_counts[s] += jnp.sum(jnp.where(here, length, 0.0).reshape(LANES // 8, 8, LANES), axis=0)

    small_lane = lane_of((chunk, LANES))

    def scan_rows(b):
        where = pl.ds(pl.multiple_of(b * chunk, chunk), chunk)
        left = columns[1, where, :] - small_lane
        shift = kept[where, 0:LANES]
        total = jnp.zeros_like(shift)
        square = jnp.zeros_like(shift)
        for t in range(1, tiles):
            d = kept[where, t * LANES : (t + 1) * LANES] - shift
            if t >= SURE:
                d = jnp.where(left > t * LANES, d, 0.0)
            total += d
            square += d * d
        count = ((left + (LANES - 1)) >> 7).astype(jnp.float32)
        off = total / count
        return shift + off, square - total * off, count

    def join_lanes(b, partial, sums):
        lane_mean, lane_square, count = partial
        where = pl.ds(pl.multiple_of(b * chunk, chunk), chunk)
        length = columns[1, where, :].astype(jnp.float32)
        mean = jnp.sum(lane_mean * count, axis=1, keepdims=True) / length
        away = lane_mean - mean
        square = jnp.sum(lane_square + count * (away * away), axis=1, keepdims=True)
        square = jnp.broadcast_to(square, mean.shape)
        slot = columns[0, where, :]
        result = []
        for s in range(PARTS):
            here = slot == small_lane + s * LANES
            for value, old in ((mean, sums[2 * s]), (square, sums[2 * s + 1])):
                put = jnp.where(here, value, 0.0).reshape(chunk // 8, 8, LANES)
                result.append(old + jnp.sum(put, axis=0))
        return tuple(result)

    zeros = tuple(jnp.zeros((8, LANES), jnp.float32) for _ in range(2 * PARTS))
    fetch(0).wait()
    first = scan_rows(0)

    def step(b, carry):
        partial, sums = carry
        fetch(b).wait()
        current = scan_rows(b)
        return current, join_lanes(b - 1, partial, sums)

    partial, sums = lax.fori_loop(1, chunks, step, (first, zeros))
    sums = join_lanes(chunks - 1, partial, sums)
    lines = []
    for s in range(PARTS):
        for piece in (sorted_ids[s], sorted_counts[s], sums[2 * s], sums[2 * s + 1]):
            lines.append(jnp.sum(piece, axis=0, keepdims=True))
    block = jnp.concatenate(lines, axis=0)
    packed[...] = block
    for peer in range(message.shape[0]):
        message[peer] = block


def own_slots(packed):
    prompt = jnp.concatenate([packed[4 * s % ROWS_MSG : 4 * s % ROWS_MSG + 1, :] for s in range(8)], axis=0)
    mean = jnp.concatenate([packed[4 * s % ROWS_MSG + 2 : 4 * s % ROWS_MSG + 3, :] for s in range(8)], axis=0)
    return prompt, mean


def match_kernel(unroll, heard, packed, found):
    pairs = heard.shape[0] // (2 * ROWS_MSG)
    prompt, mean = own_slots(packed)
    zero = jnp.zeros((8, LANES), jnp.float32)
    totals = [zero, zero, zero]
    batch = 8
    for k0 in range(0, SEG, batch):
        own = [spin(prompt, k) for k in range(k0, k0 + batch)]
        about = [spin(mean, k) for k in range(k0, k0 + batch)]

        def step(i, sums):
            sums = list(sums)
            for u in range(unroll):
                at = (i * unroll + u) * 2 * ROWS_MSG
                pid, count, center, spread = (heard[pl.ds(at + v, 8, stride=VALUES), :] for v in range(VALUES))
                for j in range(batch):
                    same = own[j] == pid
                    n = jnp.where(same, count, 0.0)
                    away = center - about[j]
                    lean = n * away
                    sums[3 * j] += n
                    sums[3 * j + 1] += lean
                    sums[3 * j + 2] += lean * away + jnp.where(same, spread, 0.0)
            return tuple(sums)

        sums = lax.fori_loop(0, pairs // unroll, step, (zero,) * (3 * batch))
        for j in range(batch):
            for v in range(3):
                totals[v] += spin(sums[3 * j + v], -(k0 + j))
    for v in range(3):
        found[v] = totals[v] + pltpu.roll(totals[v], 4, 0)


def apply_kernel(chunk, owner_ref, kept, columns, packed, found_one, found_two, heard_one, heard_two, advantage, mean_out, var_out, staged, table, sem):
    rows, width = kept.shape
    tiles = width // LANES
    chunks = rows // chunk
    small_lane = lane_of((chunk, LANES))
    _, about = own_slots(packed)
    count, lean, square = (found_one[v] + found_two[v] for v in range(3))
    off = lean / count
    var = jnp.maximum(square - lean * off, 0.0) / count
    table[0] = about + off
    table[1] = lax.rsqrt(var + EPSILON)

    def look_up(b):
        where = pl.ds(pl.multiple_of(b * chunk, chunk), chunk)
        slot = columns[0, where, :]
        mean = jnp.zeros((chunk, LANES), jnp.float32)
        scale = jnp.zeros((chunk, LANES), jnp.float32)
        for s in range(PARTS):
            here = slot == small_lane + s * LANES
            mean += jnp.where(here, table[0, s : s + 1, :], 0.0)
            scale += jnp.where(here, table[1, s : s + 1, :], 0.0)
        mean = jnp.sum(mean, axis=1, keepdims=True)
        scale = jnp.sum(scale, axis=1, keepdims=True)
        return jnp.broadcast_to(mean, (chunk, LANES)), jnp.broadcast_to(scale, (chunk, LANES))

    def send(b):
        where = pl.ds(pl.multiple_of(b * chunk, chunk), chunk)
        return pltpu.make_async_copy(staged.at[where], advantage.at[where], sem.at[b])

    def normalize(b, mean, scale):
        where = pl.ds(pl.multiple_of(b * chunk, chunk), chunk)
        left = columns[1, where, :] - small_lane
        for t in range(tiles):
            at = slice(t * LANES, (t + 1) * LANES)
            value = (kept[where, at] - mean) * scale
            if t >= SURE:
                value = jnp.where(left > t * LANES, value, 0.0)
            staged[where, at] = value
        send(b).start()

    def step(b, carry):
        later = look_up(b + 1)
        normalize(b, *carry)
        return later

    last = lax.fori_loop(0, chunks - 1, step, look_up(0))
    normalize(chunks - 1, *last)

    owner = owner_ref[0]
    part, segment = owner // 8, owner % 8
    lane = lane_of((8, LANES))
    place = segment * SEG + lane % SEG
    prompts = (owner * P_DEV + lane).astype(jnp.float32)
    blocks = []
    for heard in (heard_one, heard_two):
        for g in range(heard.shape[0] // (8 * ROWS_MSG)):
            at = g * 8 * ROWS_MSG + part * VALUES
            blocks.append(
                [jnp.take_along_axis(heard[pl.ds(at + v, 8, stride=ROWS_MSG), :], place, axis=1) for v in range(VALUES)]
            )
    zero = jnp.zeros((8, LANES), jnp.float32)
    count_all, sum_all = zero, zero
    for k in range(SEG):
        turned = spin(prompts, k)
        n_k, s_k = zero, zero
        for pid, n, center, _ in blocks:
            n = jnp.where(turned == pid, n, 0.0)
            n_k += n
            s_k += n * center
        count_all += spin(n_k, -k)
        sum_all += spin(s_k, -k)
    count_all = jnp.broadcast_to(jnp.sum(count_all, axis=0, keepdims=True), (8, LANES))
    mean_all = jnp.broadcast_to(jnp.sum(sum_all, axis=0, keepdims=True), (8, LANES)) / count_all
    spread_all = zero
    for k in range(SEG):
        turned = spin(prompts, k)
        about_k = spin(mean_all, k)
        q_k = zero
        for pid, n, center, spread in blocks:
            away = center - about_k
            q_k += jnp.where(turned == pid, spread + n * (away * away), 0.0)
        spread_all += spin(q_k, -k)
    spread_all = jnp.sum(spread_all, axis=0, keepdims=True)
    mean_out[...] = mean_all[0:1, :]
    var_out[...] = spread_all / count_all[0:1, :]

    for b in range(chunks):
        send(b).wait()


def body(rewards, lengths, prompt_ids):
    rows, width = rewards.shape
    groups = rows // LANES
    peers = 1
    for axis in CHIPS:
        peers *= lax.axis_size(axis)
    vmem = pl.BlockSpec(memory_space=pltpu.VMEM)
    hbm = pl.BlockSpec(memory_space=pltpu.HBM)
    chunk = 32
    kept, message, packed, columns = pl.pallas_call(
        lambda *refs: stats_kernel(chunk, *refs),
        out_shape=(
            pltpu.VMEM((rows, width), jnp.float32),
            pltpu.VMEM((peers, ROWS_MSG, LANES), jnp.float32),
            pltpu.VMEM((ROWS_MSG, LANES), jnp.float32),
            pltpu.VMEM((2, rows, LANES), jnp.int32),
        ),
        in_specs=[hbm, vmem, vmem],
        out_specs=(vmem, vmem, vmem, vmem),
        scratch_shapes=[pltpu.SemaphoreType.DMA((rows // chunk,))],
        compiler_params=pltpu.CompilerParams(vmem_limit_bytes=4 * MIB),
        name="row_statistics",
    )(pltpu.with_memory_space_constraint(rewards, pltpu.HBM), lengths.reshape(groups, LANES), prompt_ids.reshape(groups, LANES))

    heard_one = lax.all_to_all(message, CHIPS, 0, 0, tiled=True)
    heard_two = lax.ppermute(heard_one, "dp_2", [(0, 1), (1, 0)])

    def match(heard):
        return pl.pallas_call(
            lambda *refs: match_kernel(2, *refs),
            out_shape=pltpu.VMEM((3, 8, LANES), jnp.float32),
            in_specs=[vmem, vmem],
            out_specs=vmem,
            compiler_params=pltpu.CompilerParams(vmem_limit_bytes=4 * MIB),
            name="match",
        )(heard, packed)

    heard_one = heard_one.reshape(peers * ROWS_MSG, LANES)
    heard_two = heard_two.reshape(peers * ROWS_MSG, LANES)
    found_one = match(heard_one)
    found_two = match(heard_two)
    owner = lax.axis_index(DP).reshape(1).astype(jnp.int32)
    advantage, prompt_mean, prompt_var = pl.pallas_call(
        lambda *refs: apply_kernel(chunk, *refs),
        out_shape=(
            jax.ShapeDtypeStruct((rows, width), jnp.float32),
            jax.ShapeDtypeStruct((1, P_DEV), jnp.float32),
            jax.ShapeDtypeStruct((1, P_DEV), jnp.float32),
        ),
        in_specs=[pl.BlockSpec(memory_space=pltpu.SMEM)] + [vmem] * 7,
        out_specs=(hbm, vmem, vmem),
        scratch_shapes=[
            pltpu.VMEM((rows, width), jnp.float32),
            pltpu.VMEM((2, 8, LANES), jnp.float32),
            pltpu.SemaphoreType.DMA((rows // chunk,)),
        ],
        compiler_params=pltpu.CompilerParams(vmem_limit_bytes=16 * MIB),
        name="normalize",
    )(owner, kept, columns, packed, found_one, found_two, heard_one, heard_two)
    return advantage, prompt_mean.reshape(P_DEV), prompt_var.reshape(P_DEV)


def solution(mesh):
    split = Mesh(mesh.devices.reshape(4, 4, 2, mesh.shape["seq"]), ("dp_0", "dp_1", "dp_2", "seq"))
    placed = (P(DP_SEQ, None), P(DP_SEQ), P(DP_SEQ))
    return jax.shard_map(
        body,
        mesh=split,
        in_specs=placed,
        out_specs=(P(DP_SEQ, None), P(DP), P(DP)),
        check_vma=False,
    )
```

```python
import jax
import jax.numpy as jnp
from jax import lax
from jax.experimental import pallas as pl
from jax.experimental.pallas import tpu as pltpu
from jax.sharding import Mesh
from jax.sharding import PartitionSpec as P

P_DEV = 128
OWNERS = 32
SEG = 16
LANES = 128
DP = ("dp_0", "dp_1", "dp_2")
DP_SEQ = ("dp_0", "dp_1", "dp_2", "seq")
CHIPS = ("dp_0", "dp_1", "seq")
EPSILON = 1e-06
MIB = 1024 * 1024
TAG = 8192
SURE = 4

PARTS = 4
VALUES = 4
ROWS_MSG = PARTS * VALUES


def lane_of(shape):
    return lax.broadcasted_iota(jnp.int32, shape, len(shape) - 1)


def spin(x, k):
    k %= SEG
    if k == 0:
        return x
    near = pltpu.roll(x, LANES - k, 1)
    wrapped = pltpu.roll(x, SEG - k, 1)
    return jnp.where(lane_of(x.shape) % SEG < SEG - k, near, wrapped)


def stats_kernel(chunk, rewards, lengths_hbm, ids_hbm, kept, message, packed, columns, lengths, ids, sem, small_sem):
    rows, width = rewards.shape
    groups = rows // LANES
    tiles = width // LANES
    chunks = rows // chunk

    def fetch(b):
        where = pl.ds(pl.multiple_of(b * chunk, chunk), chunk)
        return pltpu.make_async_copy(rewards.at[where], kept.at[where], sem.at[b])

    small = (
        pltpu.make_async_copy(lengths_hbm, lengths, small_sem.at[0]),
        pltpu.make_async_copy(ids_hbm, ids, small_sem.at[1]),
    )
    for copy in small:
        copy.start()
    for b in range(2):
        fetch(b).start()
    for copy in small:
        copy.wait()
    for b in range(2, chunks):
        fetch(b).start()

    lane = lane_of((LANES, LANES))
    before = jnp.where(lax.broadcasted_iota(jnp.int32, (LANES, LANES), 0) < lane, 1.0, 0.0)
    counter = jnp.concatenate([before, jnp.ones((LANES, LANES), jnp.float32)], axis=1)
    owners = ids[...] >> 7
    each = lax.broadcasted_iota(jnp.int32, (OWNERS, LANES), 0)
    mine = [jnp.where(owners[g : g + 1, :] == each, 1.0, 0.0) for g in range(groups)]
    counts = jnp.dot(jnp.concatenate(mine, axis=0), counter, preferred_element_type=jnp.float32)
    slots = []
    so_far = jnp.zeros((OWNERS, LANES), jnp.float32)
    for g in range(groups):
        part = counts[g * OWNERS : (g + 1) * OWNERS]
        rank = jnp.sum(mine[g] * (part[:, :LANES] + so_far), axis=0, keepdims=True)
        so_far += part[:, LANES:]
        slots.append(owners[g : g + 1, :] * SEG + rank.astype(jnp.int32))
    tag = (ids[...] & (P_DEV - 1)) * TAG + lengths[...]
    turned = jnp.concatenate(slots + [tag], axis=0).astype(jnp.float32).T.astype(jnp.int32)
    for g in range(groups):
        at = slice(g * LANES, (g + 1) * LANES)
        columns[0, at, :] = jnp.broadcast_to(turned[:, g : g + 1], (LANES, LANES))
        columns[1, at, :] = jnp.broadcast_to(turned[:, groups + g : groups + g + 1], (LANES, LANES))

    small_lane = lane_of((chunk, LANES))

    def scan_rows(b):
        where = pl.ds(pl.multiple_of(b * chunk, chunk), chunk)
        left = (columns[1, where, :] & (TAG - 1)) - small_lane
        shift = kept[where, 0:LANES]
        total = jnp.zeros_like(shift)
        square = jnp.zeros_like(shift)
        for t in range(1, tiles):
            d = kept[where, t * LANES : (t + 1) * LANES] - shift
            if t >= SURE:
                d = jnp.where(left > t * LANES, d, 0.0)
            total += d
            square += d * d
        count = ((left + (LANES - 1)) >> 7).astype(jnp.float32)
        off = total / count
        return shift + off, square - total * off, count

    def join_lanes(b, partial, sums):
        lane_mean, lane_square, count = partial
        where = pl.ds(pl.multiple_of(b * chunk, chunk), chunk)
        tags = columns[1, where, :]
        length = (tags & (TAG - 1)).astype(jnp.float32)
        mean = jnp.sum(lane_mean * count, axis=1, keepdims=True) / length
        away = lane_mean - mean
        square = jnp.sum(lane_square + count * (away * away), axis=1, keepdims=True)
        square = jnp.broadcast_to(square, mean.shape)
        slot = columns[0, where, :]
        sums = list(sums)
        for s in range(PARTS):
            for r in range(0, chunk, 8):
                row = slice(r, r + 8)
                here = slot[row] == small_lane[row] + s * LANES
                for v, value in enumerate((tags, mean, square)):
                    sums[3 * s + v] = jnp.where(here, value[row], sums[3 * s + v])
        return tuple(sums)

    zeros = (jnp.zeros((8, LANES), jnp.int32), jnp.zeros((8, LANES), jnp.float32), jnp.zeros((8, LANES), jnp.float32)) * PARTS
    fetch(0).wait()
    first = scan_rows(0)

    def step(b, carry):
        partial, sums = carry
        fetch(b).wait()
        current = scan_rows(b)
        return current, join_lanes(b - 1, partial, sums)

    partial, sums = lax.fori_loop(1, chunks, step, (first, zeros))
    sums = join_lanes(chunks - 1, partial, sums)
    lines = []
    one_lane = lane_of((1, LANES))
    for s in range(PARTS):
        tags, mean, square = (jnp.sum(piece, axis=0, keepdims=True) for piece in sums[3 * s : 3 * s + 3])
        prompt = (tags >> 13) + ((s * LANES + one_lane) >> 4) * P_DEV
        lines += [prompt.astype(jnp.float32), (tags & (TAG - 1)).astype(jnp.float32), mean, square]
    block = jnp.concatenate(lines, axis=0)
    packed[...] = block
    for peer in range(message.shape[0]):
        message[peer] = block


def own_slots(packed):
    prompt = jnp.concatenate([packed[4 * s % ROWS_MSG : 4 * s % ROWS_MSG + 1, :] for s in range(8)], axis=0)
    mean = jnp.concatenate([packed[4 * s % ROWS_MSG + 2 : 4 * s % ROWS_MSG + 3, :] for s in range(8)], axis=0)
    return prompt, mean


def match_kernel(unroll, heard, packed, found):
    pairs = heard.shape[0] // (2 * ROWS_MSG)
    prompt, mean = own_slots(packed)
    zero = jnp.zeros((8, LANES), jnp.float32)
    totals = [zero, zero, zero]
    batch = 8
    for k0 in range(0, SEG, batch):
        own = [spin(prompt, k) for k in range(k0, k0 + batch)]
        about = [spin(mean, k) for k in range(k0, k0 + batch)]

        def step(i, sums):
            sums = list(sums)
            for u in range(unroll):
                at = (i * unroll + u) * 2 * ROWS_MSG
                pid, count, center, spread = (heard[pl.ds(at + v, 8, stride=VALUES), :] for v in range(VALUES))
                for j in range(batch):
                    same = own[j] == pid
                    n = jnp.where(same, count, 0.0)
                    away = center - about[j]
                    lean = n * away
                    sums[3 * j] += n
                    sums[3 * j + 1] += lean
                    sums[3 * j + 2] += lean * away + jnp.where(same, spread, 0.0)
            return tuple(sums)

        sums = lax.fori_loop(0, pairs // unroll, step, (zero,) * (3 * batch))
        for j in range(batch):
            for v in range(3):
                totals[v] += spin(sums[3 * j + v], -(k0 + j))
    for v in range(3):
        found[v] = totals[v] + pltpu.roll(totals[v], 4, 0)


def apply_kernel(chunk, kept, columns, packed, found_one, found_two, heard_one, heard_two, advantage, mean_out, var_out, staged, table, sem):
    rows, width = kept.shape
    tiles = width // LANES
    chunks = rows // chunk
    small_lane = lane_of((chunk, LANES))
    _, about = own_slots(packed)
    count, lean, square = (found_one[v] + found_two[v] for v in range(3))
    off = lean / count
    var = jnp.maximum(square - lean * off, 0.0) / count
    table[0] = about + off
    table[1] = lax.rsqrt(var + EPSILON)

    def look_up(b):
        where = pl.ds(pl.multiple_of(b * chunk, chunk), chunk)
        slot = columns[0, where, :]
        mean = jnp.zeros((chunk, LANES), jnp.float32)
        scale = jnp.zeros((chunk, LANES), jnp.float32)
        for s in range(PARTS):
            here = slot == small_lane + s * LANES
            mean += jnp.where(here, table[0, s : s + 1, :], 0.0)
            scale += jnp.where(here, table[1, s : s + 1, :], 0.0)
        mean = jnp.sum(mean, axis=1, keepdims=True)
        scale = jnp.sum(scale, axis=1, keepdims=True)
        return jnp.broadcast_to(mean, (chunk, LANES)), jnp.broadcast_to(scale, (chunk, LANES))

    def send(b):
        where = pl.ds(pl.multiple_of(b * chunk, chunk), chunk)
        return pltpu.make_async_copy(staged.at[where], advantage.at[where], sem.at[b])

    def normalize(b, mean, scale):
        where = pl.ds(pl.multiple_of(b * chunk, chunk), chunk)
        left = (columns[1, where, :] & (TAG - 1)) - small_lane
        for t in range(tiles):
            at = slice(t * LANES, (t + 1) * LANES)
            value = (kept[where, at] - mean) * scale
            if t >= SURE:
                value = jnp.where(left > t * LANES, value, 0.0)
            staged[where, at] = value
        send(b).start()

    def step(b, carry):
        later = look_up(b + 1)
        normalize(b, *carry)
        return later

    last = lax.fori_loop(0, chunks - 1, step, look_up(0))
    normalize(chunks - 1, *last)

    owner = lax.axis_index(DP)
    part, segment = owner // 8, owner % 8
    lane = lane_of((8, LANES))
    place = segment * SEG + lane % SEG
    prompts = (owner * P_DEV + lane).astype(jnp.float32)
    blocks = []
    for heard in (heard_one, heard_two):
        for g in range(heard.shape[0] // (8 * ROWS_MSG)):
            at = g * 8 * ROWS_MSG + part * VALUES
            blocks.append(
                [jnp.take_along_axis(heard[pl.ds(at + v, 8, stride=ROWS_MSG), :], place, axis=1) for v in range(VALUES)]
            )
    zero = jnp.zeros((8, LANES), jnp.float32)
    count_all, sum_all = zero, zero
    for k in range(SEG):
        turned = spin(prompts, k)
        n_k, s_k = zero, zero
        for pid, n, center, _ in blocks:
            n = jnp.where(turned == pid, n, 0.0)
            n_k += n
            s_k += n * center
        count_all += spin(n_k, -k)
        sum_all += spin(s_k, -k)
    count_all = jnp.broadcast_to(jnp.sum(count_all, axis=0, keepdims=True), (8, LANES))
    mean_all = jnp.broadcast_to(jnp.sum(sum_all, axis=0, keepdims=True), (8, LANES)) / count_all
    spread_all = zero
    for k in range(SEG):
        turned = spin(prompts, k)
        about_k = spin(mean_all, k)
        q_k = zero
        for pid, n, center, spread in blocks:
            away = center - about_k
            q_k += jnp.where(turned == pid, spread + n * (away * away), 0.0)
        spread_all += spin(q_k, -k)
    spread_all = jnp.sum(spread_all, axis=0, keepdims=True)
    mean_out[...] = mean_all[0:1, :]
    var_out[...] = spread_all / count_all[0:1, :]

    for b in range(chunks):
        send(b).wait()


def in_hbm(x):
    return pltpu.with_memory_space_constraint(x, pltpu.HBM)


def body(rewards, lengths, prompt_ids):
    rows, width = rewards.shape
    groups = rows // LANES
    peers = 1
    for axis in CHIPS:
        peers *= lax.axis_size(axis)
    vmem = pl.BlockSpec(memory_space=pltpu.VMEM)
    hbm = pl.BlockSpec(memory_space=pltpu.HBM)
    chunk = 64
    kept, message, packed, columns = pl.pallas_call(
        lambda *refs: stats_kernel(chunk, *refs),
        out_shape=(
            pltpu.VMEM((rows, width), jnp.float32),
            pltpu.VMEM((peers, ROWS_MSG, LANES), jnp.float32),
            pltpu.VMEM((ROWS_MSG, LANES), jnp.float32),
            pltpu.VMEM((2, rows, LANES), jnp.int32),
        ),
        in_specs=[hbm, hbm, hbm],
        out_specs=(vmem, vmem, vmem, vmem),
        scratch_shapes=[
            pltpu.VMEM((groups, LANES), jnp.int32),
            pltpu.VMEM((groups, LANES), jnp.int32),
            pltpu.SemaphoreType.DMA((rows // chunk,)),
            pltpu.SemaphoreType.DMA((2,)),
        ],
        compiler_params=pltpu.CompilerParams(vmem_limit_bytes=4 * MIB),
        name="row_statistics",
    )(in_hbm(rewards), in_hbm(lengths.reshape(groups, LANES)), in_hbm(prompt_ids.reshape(groups, LANES)))

    heard_one = lax.all_to_all(message, CHIPS, 0, 0, tiled=True)
    heard_two = lax.ppermute(heard_one, "dp_2", [(0, 1), (1, 0)])

    def match(heard):
        return pl.pallas_call(
            lambda *refs: match_kernel(2, *refs),
            out_shape=pltpu.VMEM((3, 8, LANES), jnp.float32),
            in_specs=[vmem, vmem],
            out_specs=vmem,
            compiler_params=pltpu.CompilerParams(vmem_limit_bytes=4 * MIB),
            name="match",
        )(heard, packed)

    heard_one = heard_one.reshape(peers * ROWS_MSG, LANES)
    heard_two = heard_two.reshape(peers * ROWS_MSG, LANES)
    found_one = match(heard_one)
    found_two = match(heard_two)
    advantage, prompt_mean, prompt_var = pl.pallas_call(
        lambda *refs: apply_kernel(chunk, *refs),
        out_shape=(
            jax.ShapeDtypeStruct((rows, width), jnp.float32),
            jax.ShapeDtypeStruct((1, P_DEV), jnp.float32),
            jax.ShapeDtypeStruct((1, P_DEV), jnp.float32),
        ),
        in_specs=[vmem] * 7,
        out_specs=(hbm, vmem, vmem),
        scratch_shapes=[
            pltpu.VMEM((rows, width), jnp.float32),
            pltpu.VMEM((2, 8, LANES), jnp.float32),
            pltpu.SemaphoreType.DMA((rows // chunk,)),
        ],
        compiler_params=pltpu.CompilerParams(vmem_limit_bytes=16 * MIB),
        name="normalize",
    )(kept, columns, packed, found_one, found_two, heard_one, heard_two)
    return advantage, prompt_mean.reshape(P_DEV), prompt_var.reshape(P_DEV)


def solution(mesh):
    split = Mesh(mesh.devices.reshape(4, 4, 2, mesh.shape["seq"]), ("dp_0", "dp_1", "dp_2", "seq"))
    placed = (P(DP_SEQ, None), P(DP_SEQ), P(DP_SEQ))
    return jax.shard_map(
        body,
        mesh=split,
        in_specs=placed,
        out_specs=(P(DP_SEQ, None), P(DP), P(DP)),
        check_vma=False,
    )
```

```python
import jax
import jax.numpy as jnp
from jax import lax
from jax.experimental import pallas as pl
from jax.experimental.pallas import tpu as pltpu
from jax.sharding import Mesh
from jax.sharding import PartitionSpec as P

P_DEV = 128
OWNERS = 32
SEG = 16
LANES = 128
DP = ("dp_0", "dp_1", "dp_2")
DP_SEQ = ("dp_0", "dp_1", "dp_2", "seq")
CHIPS = ("dp_0", "dp_1", "seq")
EPSILON = 1e-06
MIB = 1024 * 1024
TAG = 8192
TAIL = 16
HEAD = (16, 16, 32)
SURE = 4

PARTS = 4
VALUES = 4
ROWS_MSG = PARTS * VALUES


def lane_of(shape):
    return lax.broadcasted_iota(jnp.int32, shape, len(shape) - 1)


def spin(x, k):
    k %= SEG
    if k == 0:
        return x
    near = pltpu.roll(x, LANES - k, 1)
    wrapped = pltpu.roll(x, SEG - k, 1)
    return jnp.where(lane_of(x.shape) % SEG < SEG - k, near, wrapped)


def stats_kernel(chunk, rewards, lengths_hbm, ids_hbm, kept, message, packed, columns, lengths, ids, sem, small_sem):
    rows, width = rewards.shape
    groups = rows // LANES
    tiles = width // LANES
    chunks = rows // chunk

    last = (chunk - TAIL, TAIL)

    def fetch(start, count, b):
        where = pl.ds(start, count)
        return pltpu.make_async_copy(rewards.at[where], kept.at[where], sem.at[b])

    def fetch_chunk(b):
        return fetch(pl.multiple_of(b * chunk, chunk), chunk, b)

    fetches = [fetch_chunk(b) for b in range(chunks - 1)]
    fetches += [fetch(rows - chunk, last[0], chunks - 1), fetch(rows - TAIL, TAIL, chunks)]

    small = (
        pltpu.make_async_copy(lengths_hbm, lengths, small_sem.at[0]),
        pltpu.make_async_copy(ids_hbm, ids, small_sem.at[1]),
    )
    for copy in small:
        copy.start()
    for copy in fetches:
        copy.start(priority=1)
    for copy in small:
        copy.wait()

    lane = lane_of((LANES, LANES))
    before = jnp.where(lax.broadcasted_iota(jnp.int32, (LANES, LANES), 0) < lane, 1.0, 0.0)
    counter = jnp.concatenate([before, jnp.ones((LANES, LANES), jnp.float32)], axis=1)
    owners = ids[...] >> 7
    each = lax.broadcasted_iota(jnp.int32, (OWNERS, LANES), 0)
    mine = [jnp.where(owners[g : g + 1, :] == each, 1.0, 0.0) for g in range(groups)]
    counts = jnp.dot(jnp.concatenate(mine, axis=0), counter, preferred_element_type=jnp.float32)
    slots = []
    so_far = jnp.zeros((OWNERS, LANES), jnp.float32)
    for g in range(groups):
        part = counts[g * OWNERS : (g + 1) * OWNERS]
        rank = jnp.sum(mine[g] * (part[:, :LANES] + so_far), axis=0, keepdims=True)
        so_far += part[:, LANES:]
        slots.append(owners[g : g + 1, :] * SEG + rank.astype(jnp.int32))
    tag = (ids[...] & (P_DEV - 1)) * TAG + lengths[...]
    turned = jnp.concatenate(slots + [tag], axis=0).astype(jnp.float32).T.astype(jnp.int32)
    for g in range(groups):
        at = slice(g * LANES, (g + 1) * LANES)
        columns[0, at, :] = jnp.broadcast_to(turned[:, g : g + 1], (LANES, LANES))
        columns[1, at, :] = jnp.broadcast_to(turned[:, groups + g : groups + g + 1], (LANES, LANES))

    def scan_rows(start, count):
        where = pl.ds(start, count)
        left = (columns[1, where, :] & (TAG - 1)) - lane_of((count, LANES))
        shift = kept[where, 0:LANES]
        total = jnp.zeros_like(shift)
        square = jnp.zeros_like(shift)
        for t in range(1, tiles):
            d = kept[where, t * LANES : (t + 1) * LANES] - shift
            if t >= SURE:
                d = jnp.where(left > t * LANES, d, 0.0)
            total += d
            square += d * d
        number = ((left + (LANES - 1)) >> 7).astype(jnp.float32)
        off = total / number
        return shift + off, square - total * off, number

    def join_lanes(start, count, partial, sums):
        lane_mean, lane_square, number = partial
        where = pl.ds(start, count)
        tags = columns[1, where, :]
        length = (tags & (TAG - 1)).astype(jnp.float32)
        mean = jnp.sum(lane_mean * number, axis=1, keepdims=True) / length
        away = lane_mean - mean
        square = jnp.sum(lane_square + number * (away * away), axis=1, keepdims=True)
        square = jnp.broadcast_to(square, mean.shape)
        slot = columns[0, where, :]
        row_lane = lane_of((8, LANES))
        sums = list(sums)
        for s in range(PARTS):
            for r in range(0, count, 8):
                row = slice(r, r + 8)
                here = slot[row] == row_lane + s * LANES
                for v, value in enumerate((tags, mean, square)):
                    sums[3 * s + v] = jnp.where(here, value[row], sums[3 * s + v])
        return tuple(sums)

    sums = (jnp.zeros((8, LANES), jnp.int32), jnp.zeros((8, LANES), jnp.float32), jnp.zeros((8, LANES), jnp.float32)) * PARTS
    fetches[0].wait()
    partial = scan_rows(0, chunk)

    def step(b, carry):
        partial, sums = carry
        start = pl.multiple_of(b * chunk, chunk)
        fetch_chunk(b).wait()
        current = scan_rows(start, chunk)
        return current, join_lanes(pl.multiple_of(start - chunk, chunk), chunk, partial, sums)

    partial, sums = lax.fori_loop(1, chunks - 1, step, (partial, sums))
    done, size = rows - 2 * chunk, chunk
    for count, copy in zip(last, fetches[-2:]):
        copy.wait()
        current = scan_rows(done + size, count)
        sums = join_lanes(done, size, partial, sums)
        partial, done, size = current, done + size, count
    sums = join_lanes(done, size, partial, sums)
    lines = []
    one_lane = lane_of((1, LANES))
    for s in range(PARTS):
        tags, mean, square = (jnp.sum(piece, axis=0, keepdims=True) for piece in sums[3 * s : 3 * s + 3])
        prompt = (tags >> 13) + ((s * LANES + one_lane) >> 4) * P_DEV
        lines += [prompt.astype(jnp.float32), (tags & (TAG - 1)).astype(jnp.float32), mean, square]
    block = jnp.concatenate(lines, axis=0)
    packed[...] = block
    for peer in range(message.shape[0]):
        message[peer] = block


def own_slots(packed):
    prompt = jnp.concatenate([packed[4 * s % ROWS_MSG : 4 * s % ROWS_MSG + 1, :] for s in range(8)], axis=0)
    mean = jnp.concatenate([packed[4 * s % ROWS_MSG + 2 : 4 * s % ROWS_MSG + 3, :] for s in range(8)], axis=0)
    return prompt, mean


def match_kernel(unroll, heard, packed, found):
    pairs = heard.shape[0] // (2 * ROWS_MSG)
    prompt, mean = own_slots(packed)
    zero = jnp.zeros((8, LANES), jnp.float32)
    totals = [zero, zero, zero]
    batch = 8
    for k0 in range(0, SEG, batch):
        own = [spin(prompt, k) for k in range(k0, k0 + batch)]
        about = [spin(mean, k) for k in range(k0, k0 + batch)]

        def step(i, sums):
            sums = list(sums)
            for u in range(unroll):
                at = (i * unroll + u) * 2 * ROWS_MSG
                pid, count, center, spread = (heard[pl.ds(at + v, 8, stride=VALUES), :] for v in range(VALUES))
                for j in range(batch):
                    same = own[j] == pid
                    n = jnp.where(same, count, 0.0)
                    away = center - about[j]
                    lean = n * away
                    sums[3 * j] += n
                    sums[3 * j + 1] += lean
                    sums[3 * j + 2] += lean * away + jnp.where(same, spread, 0.0)
            return tuple(sums)

        sums = lax.fori_loop(0, pairs // unroll, step, (zero,) * (3 * batch))
        for j in range(batch):
            for v in range(3):
                totals[v] += spin(sums[3 * j + v], -(k0 + j))
    for v in range(3):
        found[v] = totals[v] + pltpu.roll(totals[v], 4, 0)


def apply_kernel(chunk, kept, columns, packed, found_one, found_two, heard_one, heard_two, advantage, mean_out, var_out, staged, table, own, sem, own_sem):
    rows, width = kept.shape
    tiles = width // LANES
    chunks = rows // chunk
    small_lane = lane_of((chunk, LANES))
    _, about = own_slots(packed)
    count, lean, square = (found_one[v] + found_two[v] for v in range(3))
    off = lean / count
    var = jnp.maximum(square - lean * off, 0.0) / count
    table[0] = about + off
    table[1] = lax.rsqrt(var + EPSILON)

    def look_up(b):
        where = pl.ds(pl.multiple_of(b * chunk, chunk), chunk)
        slot = columns[0, where, :]
        mean = jnp.zeros((chunk, LANES), jnp.float32)
        scale = jnp.zeros((chunk, LANES), jnp.float32)
        for s in range(PARTS):
            here = slot == small_lane + s * LANES
            mean += jnp.where(here, table[0, s : s + 1, :], 0.0)
            scale += jnp.where(here, table[1, s : s + 1, :], 0.0)
        mean = jnp.sum(mean, axis=1, keepdims=True)
        scale = jnp.sum(scale, axis=1, keepdims=True)
        return jnp.broadcast_to(mean, (chunk, LANES)), jnp.broadcast_to(scale, (chunk, LANES))

    def send(start, count, b):
        where = pl.ds(start, count)
        return pltpu.make_async_copy(staged.at[where], advantage.at[where], sem.at[b])

    def send_chunk(b):
        return send(pl.multiple_of(b * chunk, chunk), chunk, b)

    def normalize(start, count, mean, scale):
        where = pl.ds(start, count)
        left = (columns[1, where, :] & (TAG - 1)) - lane_of((count, LANES))
        for t in range(tiles):
            at = slice(t * LANES, (t + 1) * LANES)
            value = (kept[where, at] - mean) * scale
            if t >= SURE:
                value = jnp.where(left > t * LANES, value, 0.0)
            staged[where, at] = value

    mean, scale = look_up(0)
    sent = []
    at = 0
    for k, count in enumerate(HEAD):
        normalize(at, count, mean[at : at + count], scale[at : at + count])
        sent.append(send(at, count, chunks + k))
        sent[-1].start()
        at += count

    def step(b, carry):
        later = look_up(b + 1)
        normalize(pl.multiple_of(b * chunk, chunk), chunk, *carry)
        send_chunk(b).start()
        return later

    carry = lax.fori_loop(1, chunks - 1, step, look_up(1))
    normalize(rows - chunk, chunk, *carry)
    send_chunk(chunks - 1).start()

    owner = lax.axis_index(DP)
    part, segment = owner // 8, owner % 8
    lane = lane_of((8, LANES))
    place = segment * SEG + lane % SEG
    prompts = (owner * P_DEV + lane).astype(jnp.float32)
    blocks = []
    for heard in (heard_one, heard_two):
        for g in range(heard.shape[0] // (8 * ROWS_MSG)):
            at = g * 8 * ROWS_MSG + part * VALUES
            blocks.append(
                [jnp.take_along_axis(heard[pl.ds(at + v, 8, stride=ROWS_MSG), :], place, axis=1) for v in range(VALUES)]
            )
    zero = jnp.zeros((8, LANES), jnp.float32)
    count_all, sum_all = zero, zero
    for k in range(SEG):
        turned = spin(prompts, k)
        n_k, s_k = zero, zero
        for pid, n, center, _ in blocks:
            n = jnp.where(turned == pid, n, 0.0)
            n_k += n
            s_k += n * center
        count_all += spin(n_k, -k)
        sum_all += spin(s_k, -k)
    count_all = jnp.broadcast_to(jnp.sum(count_all, axis=0, keepdims=True), (8, LANES))
    mean_all = jnp.broadcast_to(jnp.sum(sum_all, axis=0, keepdims=True), (8, LANES)) / count_all
    spread_all = zero
    for k in range(SEG):
        turned = spin(prompts, k)
        about_k = spin(mean_all, k)
        q_k = zero
        for pid, n, center, spread in blocks:
            away = center - about_k
            q_k += jnp.where(turned == pid, spread + n * (away * away), 0.0)
        spread_all += spin(q_k, -k)
    spread_all = jnp.sum(spread_all, axis=0, keepdims=True)
    own[0] = mean_all[0:1, :]
    own[1] = spread_all / count_all[0:1, :]
    for k, out in enumerate((mean_out, var_out)):
        sent.append(pltpu.make_async_copy(own.at[k], out, own_sem.at[k]))
        sent[-1].start(priority=1)

    for b in range(1, chunks):
        send_chunk(b).wait()
    for copy in sent:
        copy.wait()


def in_hbm(x):
    return pltpu.with_memory_space_constraint(x, pltpu.HBM)


def body(rewards, lengths, prompt_ids):
    rows, width = rewards.shape
    groups = rows // LANES
    peers = 1
    for axis in CHIPS:
        peers *= lax.axis_size(axis)
    vmem = pl.BlockSpec(memory_space=pltpu.VMEM)
    hbm = pl.BlockSpec(memory_space=pltpu.HBM)
    chunk = 64
    kept, message, packed, columns = pl.pallas_call(
        lambda *refs: stats_kernel(chunk, *refs),
        out_shape=(
            pltpu.VMEM((rows, width), jnp.float32),
            pltpu.VMEM((peers, ROWS_MSG, LANES), jnp.float32),
            pltpu.VMEM((ROWS_MSG, LANES), jnp.float32),
            pltpu.VMEM((2, rows, LANES), jnp.int32),
        ),
        in_specs=[hbm, hbm, hbm],
        out_specs=(vmem, vmem, vmem, vmem),
        scratch_shapes=[
            pltpu.VMEM((groups, LANES), jnp.int32),
            pltpu.VMEM((groups, LANES), jnp.int32),
            pltpu.SemaphoreType.DMA((rows // chunk + 1,)),
            pltpu.SemaphoreType.DMA((2,)),
        ],
        compiler_params=pltpu.CompilerParams(vmem_limit_bytes=4 * MIB),
        name="row_statistics",
    )(in_hbm(rewards), in_hbm(lengths.reshape(groups, LANES)), in_hbm(prompt_ids.reshape(groups, LANES)))

    def swap(x):
        return lax.ppermute(x, "dp_2", [(0, 1), (1, 0)])

    heard_one = lax.all_to_all(message, CHIPS, 0, 0, tiled=True)
    heard_two = swap(heard_one)

    def match(heard):
        return pl.pallas_call(
            lambda *refs: match_kernel(8, *refs),
            out_shape=pltpu.VMEM((3, 8, LANES), jnp.float32),
            in_specs=[vmem, vmem],
            out_specs=vmem,
            compiler_params=pltpu.CompilerParams(vmem_limit_bytes=4 * MIB),
            name="match",
        )(heard, packed)

    heard_one = heard_one.reshape(peers * ROWS_MSG, LANES)
    heard_two = heard_two.reshape(peers * ROWS_MSG, LANES)
    found_one = match(heard_one)
    found_two = match(heard_two)
    advantage, prompt_mean, prompt_var = pl.pallas_call(
        lambda *refs: apply_kernel(chunk, *refs),
        out_shape=(
            pltpu.HBM((rows, width), jnp.float32),
            pltpu.HBM((1, P_DEV), jnp.float32),
            pltpu.HBM((1, P_DEV), jnp.float32),
        ),
        in_specs=[vmem] * 7,
        out_specs=(hbm, hbm, hbm),
        scratch_shapes=[
            pltpu.VMEM((rows, width), jnp.float32),
            pltpu.VMEM((2, 8, LANES), jnp.float32),
            pltpu.VMEM((2, 1, LANES), jnp.float32),
            pltpu.SemaphoreType.DMA((rows // chunk + len(HEAD),)),
            pltpu.SemaphoreType.DMA((2,)),
        ],
        compiler_params=pltpu.CompilerParams(vmem_limit_bytes=16 * MIB),
        name="normalize",
    )(kept, columns, packed, found_one, found_two, heard_one, heard_two)
    return advantage, prompt_mean.reshape(P_DEV), prompt_var.reshape(P_DEV)


def solution(mesh):
    split = Mesh(mesh.devices.reshape(4, 4, 2, mesh.shape["seq"]), ("dp_0", "dp_1", "dp_2", "seq"))
    placed = (P(DP_SEQ, None), P(DP_SEQ), P(DP_SEQ))
    return jax.shard_map(
        body,
        mesh=split,
        in_specs=placed,
        out_specs=(P(DP_SEQ, None), P(DP), P(DP)),
        check_vma=False,
    )
```

```python
import jax
import jax.numpy as jnp
from jax import lax
from jax.experimental import pallas as pl
from jax.experimental.pallas import tpu as pltpu
from jax.sharding import Mesh
from jax.sharding import PartitionSpec as P

P_DEV = 128
OWNERS = 32
SEG = 16
LANES = 128
DP = ("dp_0", "dp_1", "dp_2")
DP_SEQ = ("dp_0", "dp_1", "dp_2", "seq")
CHIPS = ("dp_0", "dp_1", "seq")
EPSILON = 1e-06
MIB = 1024 * 1024
TAG = 8192
BATCH = 8
UNROLL = 8
TAIL = 16
HEAD = (16, 16, 32)
SURE = 4

PARTS = 4
VALUES = 4
ROWS_MSG = PARTS * VALUES


def lane_of(shape):
    return lax.broadcasted_iota(jnp.int32, shape, len(shape) - 1)


def spin(x, k):
    k %= SEG
    if k == 0:
        return x
    near = pltpu.roll(x, LANES - k, 1)
    wrapped = pltpu.roll(x, SEG - k, 1)
    return jnp.where(lane_of(x.shape) % SEG < SEG - k, near, wrapped)


def stats_kernel(chunk, rewards, lengths_hbm, ids_hbm, kept, message, packed, columns, lengths, ids, sem, small_sem):
    rows, width = rewards.shape
    groups = rows // LANES
    tiles = width // LANES
    chunks = rows // chunk

    last = (chunk - TAIL, TAIL)

    def fetch(start, count, b):
        where = pl.ds(start, count)
        return pltpu.make_async_copy(rewards.at[where], kept.at[where], sem.at[b])

    def fetch_chunk(b):
        return fetch(pl.multiple_of(b * chunk, chunk), chunk, b)

    fetches = [fetch_chunk(b) for b in range(chunks - 1)]
    fetches += [fetch(rows - chunk, last[0], chunks - 1), fetch(rows - TAIL, TAIL, chunks)]

    small = (
        pltpu.make_async_copy(lengths_hbm, lengths, small_sem.at[0]),
        pltpu.make_async_copy(ids_hbm, ids, small_sem.at[1]),
    )
    for copy in small:
        copy.start()
    for copy in fetches:
        copy.start(priority=1)
    for copy in small:
        copy.wait()

    lane = lane_of((LANES, LANES))
    before = jnp.where(lax.broadcasted_iota(jnp.int32, (LANES, LANES), 0) < lane, 1.0, 0.0)
    counter = jnp.concatenate([before, jnp.ones((LANES, LANES), jnp.float32)], axis=1)
    owners = ids[...] >> 7
    each = lax.broadcasted_iota(jnp.int32, (OWNERS, LANES), 0)
    mine = [jnp.where(owners[g : g + 1, :] == each, 1.0, 0.0) for g in range(groups)]
    counts = jnp.dot(jnp.concatenate(mine, axis=0), counter, preferred_element_type=jnp.float32)
    slots = []
    so_far = jnp.zeros((OWNERS, LANES), jnp.float32)
    for g in range(groups):
        part = counts[g * OWNERS : (g + 1) * OWNERS]
        rank = jnp.sum(mine[g] * (part[:, :LANES] + so_far), axis=0, keepdims=True)
        so_far += part[:, LANES:]
        slots.append(owners[g : g + 1, :] * SEG + rank.astype(jnp.int32))
    tag = (ids[...] & (P_DEV - 1)) * TAG + lengths[...]
    turned = jnp.concatenate(slots + [tag], axis=0).astype(jnp.float32).T.astype(jnp.int32)
    for g in range(groups):
        at = slice(g * LANES, (g + 1) * LANES)
        columns[0, at, :] = jnp.broadcast_to(turned[:, g : g + 1], (LANES, LANES))
        columns[1, at, :] = jnp.broadcast_to(turned[:, groups + g : groups + g + 1], (LANES, LANES))

    def scan_rows(start, count):
        where = pl.ds(start, count)
        left = (columns[1, where, :] & (TAG - 1)) - lane_of((count, LANES))
        shift = kept[where, 0:LANES]
        total = jnp.zeros_like(shift)
        square = jnp.zeros_like(shift)
        for t in range(1, tiles):
            d = kept[where, t * LANES : (t + 1) * LANES] - shift
            if t >= SURE:
                d = jnp.where(left > t * LANES, d, 0.0)
            total += d
            square += d * d
        number = ((left + (LANES - 1)) >> 7).astype(jnp.float32)
        off = total / number
        return shift + off, square - total * off, number

    def join_lanes(start, count, partial, sums):
        lane_mean, lane_square, number = partial
        where = pl.ds(start, count)
        tags = columns[1, where, :]
        length = (tags & (TAG - 1)).astype(jnp.float32)
        mean = jnp.sum(lane_mean * number, axis=1, keepdims=True) / length
        away = lane_mean - mean
        square = jnp.sum(lane_square + number * (away * away), axis=1, keepdims=True)
        square = jnp.broadcast_to(square, mean.shape)
        slot = columns[0, where, :]
        row_lane = lane_of((8, LANES))
        sums = list(sums)
        for s in range(PARTS):
            for r in range(0, count, 8):
                row = slice(r, r + 8)
                here = slot[row] == row_lane + s * LANES
                for v, value in enumerate((tags, mean, square)):
                    sums[3 * s + v] = jnp.where(here, value[row], sums[3 * s + v])
        return tuple(sums)

    sums = (jnp.zeros((8, LANES), jnp.int32), jnp.zeros((8, LANES), jnp.float32), jnp.zeros((8, LANES), jnp.float32)) * PARTS
    fetches[0].wait()
    partial = scan_rows(0, chunk)

    def step(b, carry):
        partial, sums = carry
        start = pl.multiple_of(b * chunk, chunk)
        fetch_chunk(b).wait()
        current = scan_rows(start, chunk)
        return current, join_lanes(pl.multiple_of(start - chunk, chunk), chunk, partial, sums)

    partial, sums = lax.fori_loop(1, chunks - 1, step, (partial, sums))
    done, size = rows - 2 * chunk, chunk
    for count, copy in zip(last, fetches[-2:]):
        copy.wait()
        current = scan_rows(done + size, count)
        sums = join_lanes(done, size, partial, sums)
        partial, done, size = current, done + size, count
    sums = join_lanes(done, size, partial, sums)
    lines = []
    one_lane = lane_of((1, LANES))
    for s in range(PARTS):
        tags, mean, square = (jnp.sum(piece, axis=0, keepdims=True) for piece in sums[3 * s : 3 * s + 3])
        prompt = (tags >> 13) + ((s * LANES + one_lane) >> 4) * P_DEV
        lines += [prompt.astype(jnp.float32), (tags & (TAG - 1)).astype(jnp.float32), mean, square]
    block = jnp.concatenate(lines, axis=0)
    packed[...] = block
    for peer in range(message.shape[0]):
        message[peer] = block


def own_slots(packed):
    prompt = jnp.concatenate([packed[4 * s % ROWS_MSG : 4 * s % ROWS_MSG + 1, :] for s in range(8)], axis=0)
    mean = jnp.concatenate([packed[4 * s % ROWS_MSG + 2 : 4 * s % ROWS_MSG + 3, :] for s in range(8)], axis=0)
    return prompt, mean


def match(heard, own, about, sums, first):
    pairs = heard.shape[0] // (2 * ROWS_MSG)
    zero = jnp.zeros((8, LANES), jnp.float32)
    for k0 in range(0, SEG, BATCH):
        ids = [own[k0 + j] for j in range(BATCH)]
        means = [about[k0 + j] for j in range(BATCH)]

        def step(i, total):
            total = list(total)
            for u in range(UNROLL):
                at = (i * UNROLL + u) * 2 * ROWS_MSG
                pid, count, center, spread = (heard[pl.ds(at + v, 8, stride=VALUES), :] for v in range(VALUES))
                for j in range(BATCH):
                    same = ids[j] == pid
                    n = jnp.where(same, count, 0.0)
                    away = center - means[j]
                    lean = n * away
                    total[3 * j] += n
                    total[3 * j + 1] += lean
                    total[3 * j + 2] += lean * away + jnp.where(same, spread, 0.0)
            return tuple(total)

        start = (zero,) * (3 * BATCH) if first else tuple(sums[3 * k0 + j] for j in range(3 * BATCH))
        total = lax.fori_loop(0, pairs // UNROLL, step, start)
        for j in range(3 * BATCH):
            sums[3 * k0 + j] = total[j]


def match_kernel(heard, packed, own, about, sums):
    prompt, mean = own_slots(packed)
    for k in range(SEG):
        own[k] = spin(prompt, k)
        about[k] = spin(mean, k)
    match(heard, own, about, sums, True)


def more_kernel(heard, own, about, before, sums):
    sums[...] = before[...]
    match(heard, own, about, sums, False)


def apply_kernel(chunk, kept, columns, packed, own_ids, own_means, sums_one, heard_one, heard_two, heard_last, advantage, mean_out, var_out, staged, sums, table, own, sem, own_sem):
    rows, width = kept.shape
    tiles = width // LANES
    chunks = rows // chunk
    small_lane = lane_of((chunk, LANES))
    sums[...] = sums_one[...]
    match(heard_last, own_ids, own_means, sums, False)
    _, about = own_slots(packed)
    found = [sum(spin(sums[3 * k + v], -k) for k in range(SEG)) for v in range(3)]
    count, lean, square = (piece + pltpu.roll(piece, 4, 0) for piece in found)
    off = lean / count
    var = jnp.maximum(square - lean * off, 0.0) / count
    table[0] = about + off
    table[1] = lax.rsqrt(var + EPSILON)

    def look_up(b):
        where = pl.ds(pl.multiple_of(b * chunk, chunk), chunk)
        slot = columns[0, where, :]
        mean = jnp.zeros((chunk, LANES), jnp.float32)
        scale = jnp.zeros((chunk, LANES), jnp.float32)
        for s in range(PARTS):
            here = slot == small_lane + s * LANES
            mean += jnp.where(here, table[0, s : s + 1, :], 0.0)
            scale += jnp.where(here, table[1, s : s + 1, :], 0.0)
        mean = jnp.sum(mean, axis=1, keepdims=True)
        scale = jnp.sum(scale, axis=1, keepdims=True)
        return jnp.broadcast_to(mean, (chunk, LANES)), jnp.broadcast_to(scale, (chunk, LANES))

    def send(start, count, b):
        where = pl.ds(start, count)
        return pltpu.make_async_copy(staged.at[where], advantage.at[where], sem.at[b])

    def send_chunk(b):
        return send(pl.multiple_of(b * chunk, chunk), chunk, b)

    def normalize(start, count, mean, scale):
        where = pl.ds(start, count)
        left = (columns[1, where, :] & (TAG - 1)) - lane_of((count, LANES))
        for t in range(tiles):
            at = slice(t * LANES, (t + 1) * LANES)
            value = (kept[where, at] - mean) * scale
            if t >= SURE:
                value = jnp.where(left > t * LANES, value, 0.0)
            staged[where, at] = value

    mean, scale = look_up(0)
    sent = []
    at = 0
    for k, count in enumerate(HEAD):
        normalize(at, count, mean[at : at + count], scale[at : at + count])
        sent.append(send(at, count, chunks + k))
        sent[-1].start()
        at += count

    def step(b, carry):
        later = look_up(b + 1)
        normalize(pl.multiple_of(b * chunk, chunk), chunk, *carry)
        send_chunk(b).start()
        return later

    carry = lax.fori_loop(1, chunks - 1, step, look_up(1))
    normalize(rows - chunk, chunk, *carry)
    send_chunk(chunks - 1).start()

    owner = lax.axis_index(DP)
    part, segment = owner // 8, owner % 8
    lane = lane_of((8, LANES))
    place = segment * SEG + lane % SEG
    prompts = (owner * P_DEV + lane).astype(jnp.float32)
    blocks = []
    for heard in (heard_one, heard_two, heard_last):
        for g in range(heard.shape[0] // (8 * ROWS_MSG)):
            at = g * 8 * ROWS_MSG + part * VALUES
            blocks.append(
                [jnp.take_along_axis(heard[pl.ds(at + v, 8, stride=ROWS_MSG), :], place, axis=1) for v in range(VALUES)]
            )
    zero = jnp.zeros((8, LANES), jnp.float32)
    count_all, sum_all = zero, zero
    for k in range(SEG):
        turned = spin(prompts, k)
        n_k, s_k = zero, zero
        for pid, n, center, _ in blocks:
            n = jnp.where(turned == pid, n, 0.0)
            n_k += n
            s_k += n * center
        count_all += spin(n_k, -k)
        sum_all += spin(s_k, -k)
    count_all = jnp.broadcast_to(jnp.sum(count_all, axis=0, keepdims=True), (8, LANES))
    mean_all = jnp.broadcast_to(jnp.sum(sum_all, axis=0, keepdims=True), (8, LANES)) / count_all
    spread_all = zero
    for k in range(SEG):
        turned = spin(prompts, k)
        about_k = spin(mean_all, k)
        q_k = zero
        for pid, n, center, spread in blocks:
            away = center - about_k
            q_k += jnp.where(turned == pid, spread + n * (away * away), 0.0)
        spread_all += spin(q_k, -k)
    spread_all = jnp.sum(spread_all, axis=0, keepdims=True)
    own[0] = mean_all[0:1, :]
    own[1] = spread_all / count_all[0:1, :]
    for k, out in enumerate((mean_out, var_out)):
        sent.append(pltpu.make_async_copy(own.at[k], out, own_sem.at[k]))
        sent[-1].start(priority=1)

    for b in range(1, chunks):
        send_chunk(b).wait()
    for copy in sent:
        copy.wait()


def in_hbm(x):
    return pltpu.with_memory_space_constraint(x, pltpu.HBM)


def body(rewards, lengths, prompt_ids):
    rows, width = rewards.shape
    groups = rows // LANES
    peers = 1
    for axis in CHIPS:
        peers *= lax.axis_size(axis)
    vmem = pl.BlockSpec(memory_space=pltpu.VMEM)
    hbm = pl.BlockSpec(memory_space=pltpu.HBM)
    chunk = 64
    kept, message, packed, columns = pl.pallas_call(
        lambda *refs: stats_kernel(chunk, *refs),
        out_shape=(
            pltpu.VMEM((rows, width), jnp.float32),
            pltpu.VMEM((peers, ROWS_MSG, LANES), jnp.float32),
            pltpu.VMEM((ROWS_MSG, LANES), jnp.float32),
            pltpu.VMEM((2, rows, LANES), jnp.int32),
        ),
        in_specs=[hbm, hbm, hbm],
        out_specs=(vmem, vmem, vmem, vmem),
        scratch_shapes=[
            pltpu.VMEM((groups, LANES), jnp.int32),
            pltpu.VMEM((groups, LANES), jnp.int32),
            pltpu.SemaphoreType.DMA((rows // chunk + 1,)),
            pltpu.SemaphoreType.DMA((2,)),
        ],
        compiler_params=pltpu.CompilerParams(vmem_limit_bytes=4 * MIB),
        name="row_statistics",
    )(in_hbm(rewards), in_hbm(lengths.reshape(groups, LANES)), in_hbm(prompt_ids.reshape(groups, LANES)))

    def swap(x):
        return lax.ppermute(x, "dp_2", [(0, 1), (1, 0)])

    heard_one = lax.all_to_all(message, CHIPS, 0, 0, tiled=True)
    heard_two = swap(heard_one[: peers // 2])
    heard_last = swap(heard_one[peers // 2 :])

    heard_one = heard_one.reshape(peers * ROWS_MSG, LANES)
    heard_two = heard_two.reshape(peers // 2 * ROWS_MSG, LANES)
    heard_last = heard_last.reshape(peers // 2 * ROWS_MSG, LANES)
    own_ids, own_means, sums = pl.pallas_call(
        match_kernel,
        out_shape=(
            pltpu.VMEM((SEG, 8, LANES), jnp.float32),
            pltpu.VMEM((SEG, 8, LANES), jnp.float32),
            pltpu.VMEM((3 * SEG, 8, LANES), jnp.float32),
        ),
        in_specs=[vmem, vmem],
        out_specs=(vmem, vmem, vmem),
        compiler_params=pltpu.CompilerParams(vmem_limit_bytes=4 * MIB),
        name="match",
    )(heard_one, packed)
    sums = pl.pallas_call(
        more_kernel,
        out_shape=pltpu.VMEM((3 * SEG, 8, LANES), jnp.float32),
        in_specs=[vmem] * 4,
        out_specs=vmem,
        compiler_params=pltpu.CompilerParams(vmem_limit_bytes=4 * MIB),
        name="match_more",
    )(heard_two, own_ids, own_means, sums)
    advantage, prompt_mean, prompt_var = pl.pallas_call(
        lambda *refs: apply_kernel(chunk, *refs),
        out_shape=(
            pltpu.HBM((rows, width), jnp.float32),
            pltpu.HBM((1, P_DEV), jnp.float32),
            pltpu.HBM((1, P_DEV), jnp.float32),
        ),
        in_specs=[vmem] * 9,
        out_specs=(hbm, hbm, hbm),
        scratch_shapes=[
            pltpu.VMEM((rows, width), jnp.float32),
            pltpu.VMEM((3 * SEG, 8, LANES), jnp.float32),
            pltpu.VMEM((2, 8, LANES), jnp.float32),
            pltpu.VMEM((2, 1, LANES), jnp.float32),
            pltpu.SemaphoreType.DMA((rows // chunk + len(HEAD),)),
            pltpu.SemaphoreType.DMA((2,)),
        ],
        compiler_params=pltpu.CompilerParams(vmem_limit_bytes=16 * MIB),
        name="normalize",
    )(kept, columns, packed, own_ids, own_means, sums, heard_one, heard_two, heard_last)
    return advantage, prompt_mean.reshape(P_DEV), prompt_var.reshape(P_DEV)


def solution(mesh):
    split = Mesh(mesh.devices.reshape(4, 4, 2, mesh.shape["seq"]), ("dp_0", "dp_1", "dp_2", "seq"))
    placed = (P(DP_SEQ, None), P(DP_SEQ), P(DP_SEQ))
    return jax.shard_map(
        body,
        mesh=split,
        in_specs=placed,
        out_specs=(P(DP_SEQ, None), P(DP), P(DP)),
        check_vma=False,
    )
```

```python
import jax
import jax.numpy as jnp
from jax import lax
from jax.experimental import pallas as pl
from jax.experimental.pallas import tpu as pltpu
from jax.sharding import Mesh
from jax.sharding import PartitionSpec as P

P_DEV = 128
OWNERS = 32
SEG = 16
LANES = 128
DP = ("dp_0", "dp_1", "dp_2")
DP_SEQ = ("dp_0", "dp_1", "dp_2", "seq")
CHIPS = ("dp_0", "dp_1", "seq")
EPSILON = 1e-06
MIB = 1024 * 1024
TAG = 8192
BATCH = 8
UNROLL = 16
TAIL = 16
HEAD = (16, 16, 32)
SURE = 4

PARTS = 4
VALUES = 4
ROWS_MSG = PARTS * VALUES


def lane_of(shape):
    return lax.broadcasted_iota(jnp.int32, shape, len(shape) - 1)


def spin(x, k):
    k %= SEG
    if k == 0:
        return x
    near = pltpu.roll(x, LANES - k, 1)
    wrapped = pltpu.roll(x, SEG - k, 1)
    return jnp.where(lane_of(x.shape) % SEG < SEG - k, near, wrapped)


def stats_kernel(chunk, rewards, lengths_hbm, ids_hbm, kept, message, packed, columns, lengths, ids, sem, small_sem):
    rows, width = rewards.shape
    groups = rows // LANES
    tiles = width // LANES
    chunks = rows // chunk

    last = (chunk - TAIL, TAIL)

    def fetch(start, count, b):
        where = pl.ds(start, count)
        return pltpu.make_async_copy(rewards.at[where], kept.at[where], sem.at[b])

    def fetch_chunk(b):
        return fetch(pl.multiple_of(b * chunk, chunk), chunk, b)

    fetches = [fetch_chunk(b) for b in range(chunks - 1)]
    fetches += [fetch(rows - chunk, last[0], chunks - 1), fetch(rows - TAIL, TAIL, chunks)]

    small = (
        pltpu.make_async_copy(lengths_hbm, lengths, small_sem.at[0]),
        pltpu.make_async_copy(ids_hbm, ids, small_sem.at[1]),
    )
    for copy in small:
        copy.start()
    for copy in fetches:
        copy.start(priority=1)
    for copy in small:
        copy.wait()

    lane = lane_of((LANES, LANES))
    before = jnp.where(lax.broadcasted_iota(jnp.int32, (LANES, LANES), 0) < lane, 1.0, 0.0)
    counter = jnp.concatenate([before, jnp.ones((LANES, LANES), jnp.float32)], axis=1)
    owners = ids[...] >> 7
    each = lax.broadcasted_iota(jnp.int32, (OWNERS, LANES), 0)
    mine = [jnp.where(owners[g : g + 1, :] == each, 1.0, 0.0) for g in range(groups)]
    counts = jnp.dot(jnp.concatenate(mine, axis=0), counter, preferred_element_type=jnp.float32)
    slots = []
    so_far = jnp.zeros((OWNERS, LANES), jnp.float32)
    for g in range(groups):
        part = counts[g * OWNERS : (g + 1) * OWNERS]
        rank = jnp.sum(mine[g] * (part[:, :LANES] + so_far), axis=0, keepdims=True)
        so_far += part[:, LANES:]
        slots.append(owners[g : g + 1, :] * SEG + rank.astype(jnp.int32))
    tag = (ids[...] & (P_DEV - 1)) * TAG + lengths[...]
    turned = jnp.concatenate(slots + [tag], axis=0).astype(jnp.float32).T.astype(jnp.int32)
    for g in range(groups):
        at = slice(g * LANES, (g + 1) * LANES)
        columns[0, at, :] = jnp.broadcast_to(turned[:, g : g + 1], (LANES, LANES))
        columns[1, at, :] = jnp.broadcast_to(turned[:, groups + g : groups + g + 1], (LANES, LANES))

    def scan_rows(start, count):
        where = pl.ds(start, count)
        left = (columns[1, where, :] & (TAG - 1)) - lane_of((count, LANES))
        shift = kept[where, 0:LANES]
        total = jnp.zeros_like(shift)
        square = jnp.zeros_like(shift)
        for t in range(1, tiles):
            d = kept[where, t * LANES : (t + 1) * LANES] - shift
            if t >= SURE:
                d = jnp.where(left > t * LANES, d, 0.0)
            total += d
            square += d * d
        number = ((left + (LANES - 1)) >> 7).astype(jnp.float32)
        off = total / number
        return shift + off, square - total * off, number

    def join_lanes(start, count, partial, sums):
        lane_mean, lane_square, number = partial
        where = pl.ds(start, count)
        tags = columns[1, where, :]
        length = (tags & (TAG - 1)).astype(jnp.float32)
        mean = jnp.sum(lane_mean * number, axis=1, keepdims=True) / length
        away = lane_mean - mean
        square = jnp.sum(lane_square + number * (away * away), axis=1, keepdims=True)
        square = jnp.broadcast_to(square, mean.shape)
        slot = columns[0, where, :]
        row_lane = lane_of((8, LANES))
        sums = list(sums)
        for s in range(PARTS):
            for r in range(0, count, 8):
                row = slice(r, r + 8)
                here = slot[row] == row_lane + s * LANES
                for v, value in enumerate((tags, mean, square)):
                    sums[3 * s + v] = jnp.where(here, value[row], sums[3 * s + v])
        return tuple(sums)

    sums = (jnp.zeros((8, LANES), jnp.int32), jnp.zeros((8, LANES), jnp.float32), jnp.zeros((8, LANES), jnp.float32)) * PARTS
    fetches[0].wait()
    partial = scan_rows(0, chunk)

    def step(b, carry):
        partial, sums = carry
        start = pl.multiple_of(b * chunk, chunk)
        fetch_chunk(b).wait()
        current = scan_rows(start, chunk)
        return current, join_lanes(pl.multiple_of(start - chunk, chunk), chunk, partial, sums)

    partial, sums = lax.fori_loop(1, chunks - 1, step, (partial, sums))
    done, size = rows - 2 * chunk, chunk
    for count, copy in zip(last, fetches[-2:]):
        copy.wait()
        current = scan_rows(done + size, count)
        sums = join_lanes(done, size, partial, sums)
        partial, done, size = current, done + size, count
    sums = join_lanes(done, size, partial, sums)
    lines = []
    one_lane = lane_of((1, LANES))
    for s in range(PARTS):
        tags, mean, square = (jnp.sum(piece, axis=0, keepdims=True) for piece in sums[3 * s : 3 * s + 3])
        prompt = (tags >> 13) + ((s * LANES + one_lane) >> 4) * P_DEV
        lines += [prompt.astype(jnp.float32), (tags & (TAG - 1)).astype(jnp.float32), mean, square]
    block = jnp.concatenate(lines, axis=0)
    packed[...] = block
    for peer in range(message.shape[0]):
        message[peer] = block


def own_slots(packed):
    prompt = jnp.concatenate([packed[4 * s % ROWS_MSG : 4 * s % ROWS_MSG + 1, :] for s in range(8)], axis=0)
    mean = jnp.concatenate([packed[4 * s % ROWS_MSG + 2 : 4 * s % ROWS_MSG + 3, :] for s in range(8)], axis=0)
    return prompt, mean


def match(heard, own, about, sums, first):
    pairs = heard.shape[0] // (2 * ROWS_MSG)
    zero = jnp.zeros((8, LANES), jnp.float32)
    for k0 in range(0, SEG, BATCH):
        ids = [own[k0 + j] for j in range(BATCH)]
        means = [about[k0 + j] for j in range(BATCH)]

        def step(i, total):
            total = list(total)
            for u in range(UNROLL):
                at = (i * UNROLL + u) * 2 * ROWS_MSG
                pid, count, center, spread = (heard[pl.ds(at + v, 8, stride=VALUES), :] for v in range(VALUES))
                for j in range(BATCH):
                    same = ids[j] == pid
                    n = jnp.where(same, count, 0.0)
                    away = center - means[j]
                    lean = n * away
                    total[3 * j] += n
                    total[3 * j + 1] += lean
                    total[3 * j + 2] += lean * away + jnp.where(same, spread, 0.0)
            return tuple(total)

        start = (zero,) * (3 * BATCH) if first else tuple(sums[3 * k0 + j] for j in range(3 * BATCH))
        total = lax.fori_loop(0, pairs // UNROLL, step, start)
        for j in range(3 * BATCH):
            sums[3 * k0 + j] = total[j]


def match_kernel(heard, packed, own, about, sums):
    prompt, mean = own_slots(packed)
    for k in range(SEG):
        own[k] = spin(prompt, k)
        about[k] = spin(mean, k)
    match(heard, own, about, sums, True)


def more_kernel(heard, own, about, before, sums):
    sums[...] = before[...]
    match(heard, own, about, sums, False)


def apply_kernel(chunk, kept, columns, packed, own_ids, own_means, sums_one, heard_one, heard_two, heard_last, advantage, mean_out, var_out, staged, sums, table, own, sem, own_sem):
    rows, width = kept.shape
    tiles = width // LANES
    chunks = rows // chunk
    small_lane = lane_of((chunk, LANES))
    sums[...] = sums_one[...]
    match(heard_last, own_ids, own_means, sums, False)
    _, about = own_slots(packed)
    found = [sum(spin(sums[3 * k + v], -k) for k in range(SEG)) for v in range(3)]
    count, lean, square = (piece + pltpu.roll(piece, 4, 0) for piece in found)
    off = lean / count
    var = jnp.maximum(square - lean * off, 0.0) / count
    table[0] = about + off
    table[1] = lax.rsqrt(var + EPSILON)

    def look_up(b):
        where = pl.ds(pl.multiple_of(b * chunk, chunk), chunk)
        slot = columns[0, where, :]
        mean = jnp.zeros((chunk, LANES), jnp.float32)
        scale = jnp.zeros((chunk, LANES), jnp.float32)
        for s in range(PARTS):
            here = slot == small_lane + s * LANES
            mean += jnp.where(here, table[0, s : s + 1, :], 0.0)
            scale += jnp.where(here, table[1, s : s + 1, :], 0.0)
        mean = jnp.sum(mean, axis=1, keepdims=True)
        scale = jnp.sum(scale, axis=1, keepdims=True)
        return jnp.broadcast_to(mean, (chunk, LANES)), jnp.broadcast_to(scale, (chunk, LANES))

    def send(start, count, b):
        where = pl.ds(start, count)
        return pltpu.make_async_copy(staged.at[where], advantage.at[where], sem.at[b])

    def send_chunk(b):
        return send(pl.multiple_of(b * chunk, chunk), chunk, b)

    def normalize(start, count, mean, scale):
        where = pl.ds(start, count)
        left = (columns[1, where, :] & (TAG - 1)) - lane_of((count, LANES))
        for t in range(tiles):
            at = slice(t * LANES, (t + 1) * LANES)
            value = (kept[where, at] - mean) * scale
            if t >= SURE:
                value = jnp.where(left > t * LANES, value, 0.0)
            staged[where, at] = value

    mean, scale = look_up(0)
    sent = []
    at = 0
    for k, count in enumerate(HEAD):
        normalize(at, count, mean[at : at + count], scale[at : at + count])
        sent.append(send(at, count, chunks + k))
        sent[-1].start()
        at += count

    def step(b, carry):
        later = look_up(b + 1)
        normalize(pl.multiple_of(b * chunk, chunk), chunk, *carry)
        send_chunk(b).start()
        return later

    carry = lax.fori_loop(1, chunks - 1, step, look_up(1))
    normalize(rows - chunk, chunk, *carry)
    send_chunk(chunks - 1).start()

    owner = lax.axis_index(DP)
    part, segment = owner // 8, owner % 8
    lane = lane_of((8, LANES))
    place = segment * SEG + lane % SEG
    prompts = (owner * P_DEV + lane).astype(jnp.float32)
    blocks = []
    for heard in (heard_one, heard_two, heard_last):
        for g in range(heard.shape[0] // (8 * ROWS_MSG)):
            at = g * 8 * ROWS_MSG + part * VALUES
            blocks.append(
                [jnp.take_along_axis(heard[pl.ds(at + v, 8, stride=ROWS_MSG), :], place, axis=1) for v in range(VALUES)]
            )
    zero = jnp.zeros((8, LANES), jnp.float32)
    count_all, sum_all = zero, zero
    for k in range(SEG):
        turned = spin(prompts, k)
        n_k, s_k = zero, zero
        for pid, n, center, _ in blocks:
            n = jnp.where(turned == pid, n, 0.0)
            n_k += n
            s_k += n * center
        count_all += spin(n_k, -k)
        sum_all += spin(s_k, -k)
    count_all = jnp.broadcast_to(jnp.sum(count_all, axis=0, keepdims=True), (8, LANES))
    mean_all = jnp.broadcast_to(jnp.sum(sum_all, axis=0, keepdims=True), (8, LANES)) / count_all
    spread_all = zero
    for k in range(SEG):
        turned = spin(prompts, k)
        about_k = spin(mean_all, k)
        q_k = zero
        for pid, n, center, spread in blocks:
            away = center - about_k
            q_k += jnp.where(turned == pid, spread + n * (away * away), 0.0)
        spread_all += spin(q_k, -k)
    spread_all = jnp.sum(spread_all, axis=0, keepdims=True)
    own[0] = mean_all[0:1, :]
    own[1] = spread_all / count_all[0:1, :]
    for k, out in enumerate((mean_out, var_out)):
        sent.append(pltpu.make_async_copy(own.at[k], out, own_sem.at[k]))
        sent[-1].start(priority=1)

    for b in range(1, chunks):
        send_chunk(b).wait()
    for copy in sent:
        copy.wait()


def in_hbm(x):
    return pltpu.with_memory_space_constraint(x, pltpu.HBM)


def body(rewards, lengths, prompt_ids):
    rows, width = rewards.shape
    groups = rows // LANES
    peers = 1
    for axis in CHIPS:
        peers *= lax.axis_size(axis)
    vmem = pl.BlockSpec(memory_space=pltpu.VMEM)
    hbm = pl.BlockSpec(memory_space=pltpu.HBM)
    chunk = 64
    kept, message, packed, columns = pl.pallas_call(
        lambda *refs: stats_kernel(chunk, *refs),
        out_shape=(
            pltpu.VMEM((rows, width), jnp.float32),
            pltpu.VMEM((peers, ROWS_MSG, LANES), jnp.float32),
            pltpu.VMEM((ROWS_MSG, LANES), jnp.float32),
            pltpu.VMEM((2, rows, LANES), jnp.int32),
        ),
        in_specs=[hbm, hbm, hbm],
        out_specs=(vmem, vmem, vmem, vmem),
        scratch_shapes=[
            pltpu.VMEM((groups, LANES), jnp.int32),
            pltpu.VMEM((groups, LANES), jnp.int32),
            pltpu.SemaphoreType.DMA((rows // chunk + 1,)),
            pltpu.SemaphoreType.DMA((2,)),
        ],
        compiler_params=pltpu.CompilerParams(vmem_limit_bytes=4 * MIB),
        name="row_statistics",
    )(in_hbm(rewards), in_hbm(lengths.reshape(groups, LANES)), in_hbm(prompt_ids.reshape(groups, LANES)))

    def swap(x):
        return lax.ppermute(x, "dp_2", [(0, 1), (1, 0)])

    heard_one = lax.all_to_all(message, CHIPS, 0, 0, tiled=True)
    heard_two = swap(heard_one[: peers // 2])
    heard_last = swap(heard_one[peers // 2 :])

    heard_one = heard_one.reshape(peers * ROWS_MSG, LANES)
    heard_two = heard_two.reshape(peers // 2 * ROWS_MSG, LANES)
    heard_last = heard_last.reshape(peers // 2 * ROWS_MSG, LANES)
    own_ids, own_means, sums = pl.pallas_call(
        match_kernel,
        out_shape=(
            pltpu.VMEM((SEG, 8, LANES), jnp.float32),
            pltpu.VMEM((SEG, 8, LANES), jnp.float32),
            pltpu.VMEM((3 * SEG, 8, LANES), jnp.float32),
        ),
        in_specs=[vmem, vmem],
        out_specs=(vmem, vmem, vmem),
        compiler_params=pltpu.CompilerParams(vmem_limit_bytes=4 * MIB),
        name="match",
    )(heard_one, packed)
    sums = pl.pallas_call(
        more_kernel,
        out_shape=pltpu.VMEM((3 * SEG, 8, LANES), jnp.float32),
        in_specs=[vmem] * 4,
        out_specs=vmem,
        compiler_params=pltpu.CompilerParams(vmem_limit_bytes=4 * MIB),
        name="match_more",
    )(heard_two, own_ids, own_means, sums)
    advantage, prompt_mean, prompt_var = pl.pallas_call(
        lambda *refs: apply_kernel(chunk, *refs),
        out_shape=(
            pltpu.HBM((rows, width), jnp.float32),
            pltpu.HBM((1, P_DEV), jnp.float32),
            pltpu.HBM((1, P_DEV), jnp.float32),
        ),
        in_specs=[vmem] * 9,
        out_specs=(hbm, hbm, hbm),
        scratch_shapes=[
            pltpu.VMEM((rows, width), jnp.float32),
            pltpu.VMEM((3 * SEG, 8, LANES), jnp.float32),
            pltpu.VMEM((2, 8, LANES), jnp.float32),
            pltpu.VMEM((2, 1, LANES), jnp.float32),
            pltpu.SemaphoreType.DMA((rows // chunk + len(HEAD),)),
            pltpu.SemaphoreType.DMA((2,)),
        ],
        compiler_params=pltpu.CompilerParams(vmem_limit_bytes=16 * MIB),
        name="normalize",
    )(kept, columns, packed, own_ids, own_means, sums, heard_one, heard_two, heard_last)
    return advantage, prompt_mean.reshape(P_DEV), prompt_var.reshape(P_DEV)


def solution(mesh):
    split = Mesh(mesh.devices.reshape(4, 4, 2, mesh.shape["seq"]), ("dp_0", "dp_1", "dp_2", "seq"))
    placed = (P(DP_SEQ, None), P(DP_SEQ), P(DP_SEQ))
    return jax.shard_map(
        body,
        mesh=split,
        in_specs=placed,
        out_specs=(P(DP_SEQ, None), P(DP), P(DP)),
        check_vma=False,
    )
```
